512 devices in a mesh: blk: 64 (over z, y_hi, core), tensor: 8 (over y_lo, x).
Axes of the slice: x: 4, y: 4 (y_hi: 2, y_lo: 2; y = y_hi * 2 + y_lo), z: 16, core: 2. Of those that a mesh axis runs over, the one named last changes fastest.
Arguments:
- weights: bfloat16 [64, 2048, 1024], P('blk', None, 'tensor')
- grads: bfloat16 [64, 2048, 1024], P('blk', None, 'tensor'), may hold values from -6 to 6
- first_moment: float32 [64, 2048, 1024], P('blk', None, 'tensor'), may hold values from -6 to 6
- second_moment: float32 [64, 2048, 1024], P('blk', None, 'tensor'), may hold values from 0.02 to 2
- vectors: bfloat16 [64, 16, 1024], P('blk', None, 'tensor'), may hold values from -6 to 6
Outputs:
- new_weights: bfloat16 [64, 2048, 1024], P('blk', None, 'tensor')
- next_vectors: float32 [64, 16, 1024], P('blk', None, 'tensor')
The draws below stay inside these ranges and needn't reach their ends.
All inputs are finite; a program needn't handle non-finite values.
Results may differ from the reference program's by a relative error of at most 0.004.
Values may be sent and summed in bfloat16 or wider, within the bound.
No kernel may reach another device: no remote copies, remote signals or barrier semaphores. Data moves between devices by JAX's collectives and lax.ppermute only.
A program may use at most 64 MiB of HBM per device.

```python
import math
import jax
import jax.numpy as jnp
from jax import lax

DW = 2048
KVW = 1024
RANK = 16
N_BLK = 64


def draw_weights(key, part):
    key = jax.random.fold_in(key, 11)
    shared_key, own_key = jax.random.split(key, 2)
    row_key, col_key = jax.random.split(shared_key, 2)
    lowest = 0.3
    row_scale = jnp.exp(jax.random.uniform(row_key, (1, DW, 1), jnp.float32, math.log(lowest), 0.0))
    col_scale = jnp.exp(jax.random.uniform(col_key, (1, 1, KVW), jnp.float32, math.log(lowest), 0.0))
    noise = jax.random.normal(own_key, (N_BLK, DW, KVW), jnp.float32)
    values = row_scale * col_scale * noise
    return values.astype(jnp.bfloat16)


def steps_of(key, extent, shards, smallest, high):
    level = 1.0
    for position, shards_of in shards:
        steps = jax.random.uniform(jax.random.fold_in(jax.random.fold_in(key, 6), position), (shards_of,), jnp.float32, smallest / len(shards), high / len(shards))
        level = level * jnp.repeat(jnp.exp(steps), extent[position] // shards_of).reshape((-1,) + (1,) * (len(extent) - 1 - position))
    return level


def gaussian(key, extent, spread, bound, pieces=(), dtype=jnp.bfloat16):
    result = spread * jax.random.normal(key, extent, jnp.float32)
    if pieces:
        result = result * steps_of(key, extent, pieces, -0.22, 0.18)
    return jnp.clip(result, -bound, bound).astype(dtype)


def setup_inputs(seed: int = 0) -> dict:
    key_of = jax.random.split(jax.random.key(seed), 6)
    return {
        "weights": draw_weights(jax.random.fold_in(key_of[5], 71), 0),
        "grads": gaussian(key_of[1], (N_BLK, DW, KVW), 1.0, 6.0, ((0, 64), (2, 8))),
        "first_moment": gaussian(key_of[2], (N_BLK, DW, KVW), 1.0, 6.0, ((0, 64), (2, 8)), jnp.float32),
        "second_moment": jnp.clip(jnp.exp(math.log(2.0) - 4.6051702 * jax.random.uniform(key_of[3], (N_BLK, DW, KVW), jnp.float32) ** steps_of(key_of[3], (N_BLK, DW, KVW), ((0, 64), (2, 8)), -0.2, 0.2)), 0.02, 2.0),
        "vectors": gaussian(key_of[4], (N_BLK, RANK, KVW), 1.0, 6.0, ((0, 64), (2, 8))),
    }


learn_rate = 0.05
beta_one = 0.9
beta_two = 0.95
epsilon = 1e-08
decay_rate = 0.1
gossip_rate = 0.5
bias_one = 1.0 - 0.9 ** 10
bias_two = 1.0 - 0.95 ** 10

def orthonormal(block):
    gram = jnp.dot(block, block.T, precision=lax.Precision.HIGHEST)
    factor = jnp.linalg.cholesky(gram)
    return jax.scipy.linalg.solve_triangular(factor, block, lower=True)

def reference(weights, grads, first_moment, second_moment, vectors):
    rank = vectors.shape[1]
    left_q = jnp.roll(vectors, 1, axis=0)

    def project(item):
        weight, q_left, q_right = item
        both = jnp.concatenate([q_left, q_right], 0)
        return lax.dot_general(both.astype(jnp.float32), weight.astype(jnp.float32), (((1,), (1,)), ((), ())), preferred_element_type=jnp.float32)
    products = lax.map(project, (weights, left_q, vectors))
    differences = products[:, rank:] - jnp.roll(products, -1, axis=0)[:, :rank]
    basis = jax.vmap(orthonormal)(differences).astype(jnp.bfloat16)
    left_basis = jnp.roll(basis, 1, axis=0)

    def image(item):
        weight, b_left, b_right = item
        both = jnp.concatenate([b_left, b_right], 0)
        return jnp.dot(both.astype(jnp.float32), weight.astype(jnp.float32), preferred_element_type=jnp.float32)
    images = lax.map(image, (weights, left_basis, basis))
    next_vectors = images[:, rank:] - jnp.roll(images, -1, axis=0)[:, :rank]
    left_next = jnp.roll(next_vectors, 1, axis=0)

    def update(item):
        weight, grad, moment_a, moment_b, b_left, b_right, n_left, n_right = item
        signed = jnp.concatenate([b_right.astype(jnp.float32), -b_left.astype(jnp.float32)], 0)
        nexts = jnp.concatenate([n_right, n_left], 0)
        correction = lax.dot_general(signed, nexts, (((0,), (0,)), ((), ())), precision=lax.Precision.HIGHEST)
        wide = weight.astype(jnp.float32)
        gfull = grad.astype(jnp.float32)
        first = beta_one * moment_a + (1.0 - beta_one) * gfull
        second = beta_two * moment_b + (1.0 - beta_two) * gfull * gfull
        step = first / bias_one / (jnp.sqrt(second / bias_two) + epsilon) + decay_rate * wide
        return (wide - learn_rate * step - gossip_rate * correction).astype(jnp.bfloat16)
    new_weights = lax.map(update, (weights, grads, first_moment, second_moment, left_basis, basis, left_next, next_vectors))
    return (new_weights, next_vectors)
```

```python
import jax
import jax.numpy as jnp
from jax import lax
from jax.experimental import pallas as pl
from jax.experimental.pallas import tpu as pltpu
from jax.sharding import PartitionSpec as P

learn_rate = 0.05
beta_one = 0.9
beta_two = 0.95
epsilon = 1e-08
decay_rate = 0.1
gossip_rate = 0.5
bias_one = 1.0 - 0.9**10
bias_two = 1.0 - 0.95**10

f32 = jnp.float32
bf16 = jnp.bfloat16


def dot(a, b, dims):
    return lax.dot_general(a, b, (dims, ((), ())), preferred_element_type=f32)


def swapped(value, axis, first):
    count = lax.axis_size(axis)
    pairs = []
    for low in range(first, first + count, 2):
        a, b = low % count, (low + 1) % count
        pairs += [(a, b), (b, a)]
    return lax.ppermute(value, axis, pairs)


def shifted(value, axis, steps):
    count = lax.axis_size(axis)
    pairs = [(source, (source + steps) % count) for source in range(count)]
    return lax.ppermute(value, axis, pairs)


def partial_kernel(w_ref, wa_ref, wb_ref, qa_ref, qb_ref, out_ref):
    qa, qb = qa_ref[...], qb_ref[...]
    zero = jnp.zeros_like(qa)
    lhs = jnp.concatenate(
        [
            jnp.concatenate([qa, -qa, zero], 1),
            jnp.concatenate([qb, zero, -qb], 1),
        ],
        0,
    )
    tile = 512
    for start in range(0, w_ref.shape[0], tile):
        rows = pl.ds(start, tile)
        rhs = jnp.concatenate([w_ref[rows], wa_ref[rows], wb_ref[rows]], 1)
        part = dot(lhs, rhs, ((1,), (1,))).astype(bf16)
        for copy in range(out_ref.shape[0]):
            out_ref[copy, :, rows] = part


def inverse_factor(gram_a, gram_b):
    rank = gram_a.shape[0]
    shape = (rank, 128)
    lane = lax.broadcasted_iota(jnp.int32, shape, 1)
    row = lax.broadcasted_iota(jnp.int32, shape, 0)
    is_a = (lane // rank) % 2 == 0
    left = []
    for j in range(rank):
        col_a = jnp.broadcast_to(gram_a[:, j : j + 1], shape)
        col_b = jnp.broadcast_to(gram_b[:, j : j + 1], shape)
        left.append(jnp.where(is_a, col_a, col_b))
    right = [jnp.where(row == j, 1.0, 0.0).astype(f32) for j in range(rank)]
    pivots = jnp.ones(shape, f32)
    for k in range(rank):
        pivot = jnp.broadcast_to(left[k][k : k + 1], shape)
        pivots = jnp.where(row == k, pivot, pivots)
        if k == rank - 1:
            break
        factor = jnp.where(row > k, left[k] / pivot, 0.0)
        for j in range(k + 1, rank):
            left[j] = left[j] - factor * jnp.broadcast_to(left[j][k : k + 1], shape)
        for j in range(k):
            right[j] = right[j] - factor * jnp.broadcast_to(right[j][k : k + 1], shape)
        right[k] = right[k] - factor
    gathered = jnp.zeros(shape, f32)
    for j in range(rank):
        gathered = jnp.where(lane % rank == j, right[j], gathered)
    return gathered / jnp.sqrt(pivots)


def finish_kernel(odd_ref, g_ref, w_ref, wa_ref, wb_ref, pre_ref, new_ref, next_ref):
    rank = next_ref.shape[0]
    diff = g_ref[0].astype(f32)
    for peer in range(1, g_ref.shape[0]):
        diff = diff + g_ref[peer].astype(f32)
    high = diff.astype(bf16)
    low = (diff - high.astype(f32)).astype(bf16)
    gram = (
        dot(high, high, ((1,), (1,)))
        + dot(high, low, ((1,), (1,)))
        + dot(low, high, ((1,), (1,)))
    )
    inverse = inverse_factor(gram[:rank, :rank], gram[rank:, rank : 2 * rank])
    lane = lax.broadcasted_iota(jnp.int32, inverse.shape, 1)
    is_a = (lane // rank) % 2 == 0
    coarse = inverse.astype(bf16).astype(f32)
    terms = jnp.where(lane < 4 * rank, coarse, inverse - coarse)
    mix = jnp.concatenate(
        [jnp.where(is_a, terms, 0.0), jnp.where(is_a, 0.0, terms)], 0
    ).astype(bf16)
    basis = dot(mix, jnp.concatenate([high, low, high, low], 0), ((1,), (0,))).astype(bf16)
    own = dot(basis, w_ref[...], ((1,), (0,)))
    next_a = own[:rank] - dot(basis[:rank], wa_ref[...], ((1,), (0,)))
    next_b = own[rank:] - dot(basis[rank:], wb_ref[...], ((1,), (0,)))
    next_ref[...] = jnp.where(odd_ref[0] == 1, next_b, next_a)
    nexts = jnp.concatenate([next_a, next_b], 0)
    one = nexts.astype(bf16)
    rest = nexts - one.astype(f32)
    two = rest.astype(bf16)
    three = (rest - two.astype(f32)).astype(bf16)
    nexts = jnp.concatenate([one, two, three], 0)
    tile = 512
    for start in range(0, w_ref.shape[0], tile):
        cols = basis[:, start : start + tile]
        lhs = jnp.concatenate([cols, cols, cols], 0)
        correction = dot(lhs, nexts, ((0,), (0,)))
        rows = pl.ds(start, tile)
        new_ref[rows] = (pre_ref[rows] - gossip_rate * correction).astype(bf16)


def body(weights, grads, first_moment, second_moment, vectors):
    weight = weights[0]
    own_q = vectors[0]
    rows, cols = weight.shape
    rank = own_q.shape[0]
    peers = lax.axis_size("tensor")
    odd = lax.axis_index("blk") % 2 == 1
    w_b = swapped(weight, "blk", 1)
    w_a = swapped(weight, "blk", 0)
    left_q = shifted(own_q, "blk", 1)
    q_a = jnp.where(odd, left_q, own_q)
    q_b = jnp.where(odd, own_q, left_q)

    wide = weight.astype(f32)
    gfull = grads[0].astype(f32)
    first = beta_one * first_moment[0] + (1.0 - beta_one) * gfull
    second = beta_two * second_moment[0] + (1.0 - beta_two) * gfull * gfull
    step = first / bias_one / (jnp.sqrt(second / bias_two) + epsilon) + decay_rate * wide
    pre = wide - learn_rate * step

    vmem = pl.BlockSpec(memory_space=pltpu.VMEM)
    params = pltpu.CompilerParams(vmem_limit_bytes=32 * 1024 * 1024)
    partials = pl.pallas_call(
        partial_kernel,
        out_shape=jax.ShapeDtypeStruct((peers, 2 * rank, rows), bf16),
        in_specs=[vmem] * 5,
        out_specs=vmem,
        compiler_params=params,
        name="partial_differences",
    )(weight, w_a, w_b, q_a, q_b)
    gathered = lax.all_to_all(partials, "tensor", 0, 0)
    new, next_right = pl.pallas_call(
        finish_kernel,
        out_shape=(
            jax.ShapeDtypeStruct((rows, cols), bf16),
            jax.ShapeDtypeStruct((rank, cols), f32),
        ),
        in_specs=[pl.BlockSpec(memory_space=pltpu.SMEM)] + [vmem] * 5,
        out_specs=(vmem, vmem),
        compiler_params=params,
        name="finish",
    )(odd.astype(jnp.int32)[None], gathered, weight, w_a, w_b, pre)
    return (new[None], next_right[None])


def solution(mesh):
    spec = P("blk", None, "tensor")
    return jax.shard_map(
        body,
        mesh=mesh,
        in_specs=(spec,) * 5,
        out_specs=(spec, spec),
        check_vma=False,
    )
```

```python
import jax
import jax.numpy as jnp
from jax import lax
from jax.experimental import pallas as pl
from jax.experimental.pallas import tpu as pltpu
from jax.sharding import PartitionSpec as P

learn_rate = 0.05
beta_one = 0.9
beta_two = 0.95
epsilon = 1e-08
decay_rate = 0.1
gossip_rate = 0.5
bias_one = 1.0 - 0.9**10
bias_two = 1.0 - 0.95**10

f32 = jnp.float32
bf16 = jnp.bfloat16


def dot(a, b, dims):
    return lax.dot_general(a, b, (dims, ((), ())), preferred_element_type=f32)


def shifted(value, axis, steps):
    count = lax.axis_size(axis)
    pairs = [(source, (source + steps) % count) for source in range(count)]
    return lax.ppermute(value, axis, pairs)


def product_kernel(w_hbm, q_hbm, pack_ref, w_ref, q_ref, sems):
    width, cols = w_ref.shape
    half = width // 2
    halves = [pl.ds(0, half), pl.ds(half, half)]
    copies = [pltpu.make_async_copy(q_hbm, q_ref, sems.at[2])]
    for i, rows in enumerate(halves):
        copies.append(pltpu.make_async_copy(w_hbm.at[rows], w_ref.at[rows], sems.at[i]))
    for copy in copies:
        copy.start()
    copies[0].wait()
    q = q_ref[...]
    pack_ref[:, pl.ds(width, cols)] = q.astype(f32)
    for i, rows in enumerate(halves):
        copies[i + 1].wait()
        pack_ref[:, rows] = dot(q, w_ref[rows], ((1,), (1,)))


def partial_kernel(pack_ref, w_ref, out_ref):
    width, cols = w_ref.shape
    q = pack_ref[:, pl.ds(width, cols)].astype(bf16)
    tile = 512
    for start in range(0, width, tile):
        rows = pl.ds(start, tile)
        w = w_ref[rows]
        part = (pack_ref[:, rows] - dot(q, w, ((1,), (1,)))).astype(bf16)
        for copy in range(out_ref.shape[0]):
            out_ref[copy, :, rows] = part


def inverse_factor(gram):
    rank = gram.shape[0]
    shape = (rank, 128)
    lane = lax.broadcasted_iota(jnp.int32, shape, 1)
    row = lax.broadcasted_iota(jnp.int32, shape, 0)
    left = [jnp.broadcast_to(gram[:, j : j + 1], shape) for j in range(rank)]
    right = [jnp.zeros(shape, f32) for j in range(rank)]
    pivots = jnp.ones(shape, f32)
    for k in range(rank):
        pivot = jnp.broadcast_to(left[k][k : k + 1], shape)
        pivots = jnp.where(row == k, pivot, pivots)
        right[k] = jnp.where(row == k, 1.0, 0.0).astype(f32)
        if k == rank - 1:
            break
        factor = jnp.where(row > k, left[k] / pivot, 0.0)
        for j in range(k + 1, rank):
            left[j] = left[j] - factor * jnp.broadcast_to(left[j][k : k + 1], shape)
        for j in range(k):
            right[j] = right[j] - factor * jnp.broadcast_to(right[j][k : k + 1], shape)
        right[k] = right[k] - factor
    gathered = jnp.zeros(shape, f32)
    for j in range(rank):
        gathered = jnp.where(lane % rank == j, right[j], gathered)
    return gathered / jnp.sqrt(pivots)


def basis_kernel(g_ref, basis_ref):
    rank = basis_ref.shape[0]
    diff = g_ref[0].astype(f32)
    for peer in range(1, g_ref.shape[0]):
        diff = diff + g_ref[peer].astype(f32)
    high = diff.astype(bf16)
    low = (diff - high.astype(f32)).astype(bf16)
    gram = (
        dot(high, high, ((1,), (1,)))
        + dot(high, low, ((1,), (1,)))
        + dot(low, high, ((1,), (1,)))
    )
    inverse = inverse_factor(gram)
    lane = lax.broadcasted_iota(jnp.int32, inverse.shape, 1)
    coarse = inverse.astype(bf16).astype(f32)
    mix = jnp.where(lane < 2 * rank, coarse, inverse - coarse)[:, : 4 * rank].astype(bf16)
    terms = jnp.concatenate([high, low, high, low], 0)
    basis_ref[...] = dot(mix, terms, ((1,), (0,))).astype(bf16)


def image_kernel(basis_ref, wl_ref, w_ref, pack_ref):
    width, cols = w_ref.shape
    basis = basis_ref[...]
    pack_ref[:, :width] = basis
    image = dot(basis, wl_ref[...], ((1,), (0,))) - dot(basis, w_ref[...], ((1,), (0,)))
    for term in range(3):
        piece = image.astype(bf16)
        pack_ref[:, pl.ds(width + term * cols, cols)] = piece
        image = image - piece.astype(f32)


def update_kernel(left_ref, right_ref, pre_ref, new_hbm, next_hbm, new_ref, next_ref, sems):
    width, cols = new_ref.shape
    terms = [pl.ds(width + term * cols, cols) for term in range(3)]
    pieces = [right_ref[:, t] for t in terms]
    next_ref[...] = (
        pieces[0].astype(f32) + pieces[1].astype(f32) + pieces[2].astype(f32)
    )
    copies = [pltpu.make_async_copy(next_ref, next_hbm, sems.at[0])]
    copies[0].start()
    nexts = jnp.concatenate(pieces + [-left_ref[:, t] for t in terms], 0)
    tile = 512
    for start in range(0, width, tile):
        rows = pl.ds(start, tile)
        left, right = left_ref[:, rows], right_ref[:, rows]
        lhs = jnp.concatenate([right, right, right, left, left, left], 0)
        correction = dot(lhs, nexts, ((0,), (0,)))
        new_ref[rows] = (pre_ref[rows] - gossip_rate * correction).astype(bf16)
        copies.append(
            pltpu.make_async_copy(new_ref.at[rows], new_hbm.at[rows], sems.at[len(copies)])
        )
        copies[-1].start()
    for copy in copies:
        copy.wait()


def body(weights, grads, first_moment, second_moment, vectors):
    weight = weights[0]
    rows, cols = weight.shape
    rank = vectors.shape[1]
    peers = lax.axis_size("tensor")
    vmem = pl.BlockSpec(memory_space=pltpu.VMEM)
    hbm = pl.BlockSpec(memory_space=pltpu.HBM)
    shaped = jax.ShapeDtypeStruct

    def call(kernel, name, out_shape, *operands):
        return pl.pallas_call(
            kernel,
            out_shape=out_shape,
            in_specs=[vmem] * len(operands),
            out_specs=jax.tree.map(lambda _: vmem, out_shape),
            compiler_params=pltpu.CompilerParams(vmem_limit_bytes=8 * 1024 * 1024),
            cost_estimate=pl.CostEstimate(
                flops=10_000_000, bytes_accessed=4_000_000, transcendentals=500_000
            ),
            name=name,
        )(*operands)

    product, w_here = pl.pallas_call(
        product_kernel,
        out_shape=(shaped((rank, rows + cols), f32), shaped((rows, cols), bf16)),
        in_specs=[hbm, hbm],
        out_specs=(vmem, vmem),
        scratch_shapes=[pltpu.VMEM((rank, cols), bf16), pltpu.SemaphoreType.DMA((3,))],
        compiler_params=pltpu.CompilerParams(vmem_limit_bytes=8 * 1024 * 1024),
        cost_estimate=pl.CostEstimate(
            flops=10_000_000, bytes_accessed=4_000_000, transcendentals=0
        ),
        name="own_product",
    )(
        pltpu.with_memory_space_constraint(weight, pltpu.HBM),
        pltpu.with_memory_space_constraint(vectors[0], pltpu.HBM),
    )
    left_product = shifted(product, "blk", 1)
    w_left = shifted(weight, "blk", 1)
    partials = call(
        partial_kernel,
        "partial_differences",
        shaped((peers, rank, rows), bf16),
        left_product,
        w_here,
    )
    gathered = lax.all_to_all(partials, "tensor", 0, 0)
    basis = call(basis_kernel, "basis", shaped((rank, rows), bf16), gathered)
    pack = call(
        image_kernel, "image", shaped((rank, rows + 3 * cols), bf16), basis, w_left, w_here
    )
    right_pack = shifted(pack, "blk", -1)

    wide = w_here.astype(f32)
    gfull = grads[0].astype(f32)
    first = beta_one * first_moment[0] + (1.0 - beta_one) * gfull
    second = beta_two * second_moment[0] + (1.0 - beta_two) * gfull * gfull
    step = first / bias_one / (jnp.sqrt(second / bias_two) + epsilon) + decay_rate * wide
    pre = wide - learn_rate * step

    new, next_right = pl.pallas_call(
        update_kernel,
        out_shape=(shaped((rows, cols), bf16), shaped((rank, cols), f32)),
        in_specs=[vmem] * 3,
        out_specs=(hbm, hbm),
        scratch_shapes=[
            pltpu.VMEM((rows, cols), bf16),
            pltpu.VMEM((rank, cols), f32),
            pltpu.SemaphoreType.DMA((1 + rows // 512,)),
        ],
        compiler_params=pltpu.CompilerParams(vmem_limit_bytes=8 * 1024 * 1024),
        cost_estimate=pl.CostEstimate(
            flops=10_000_000, bytes_accessed=4_000_000, transcendentals=0
        ),
        name="update",
    )(pack, right_pack, pre)
    return (new[None], next_right[None])


def solution(mesh):
    spec = P("blk", None, "tensor")
    return jax.shard_map(
        body,
        mesh=mesh,
        in_specs=(spec,) * 5,
        out_specs=(spec, spec),
        check_vma=False,
    )
```

```python
import jax
import jax.numpy as jnp
from jax import lax
from jax.experimental import pallas as pl
from jax.experimental.pallas import tpu as pltpu
from jax.sharding import PartitionSpec as P

learn_rate = 0.05
beta_one = 0.9
beta_two = 0.95
epsilon = 1e-08
decay_rate = 0.1
gossip_rate = 0.5
bias_one = 1.0 - 0.9**10
bias_two = 1.0 - 0.95**10

f32 = jnp.float32
bf16 = jnp.bfloat16


def dot(a, b, dims):
    return lax.dot_general(a, b, (dims, ((), ())), preferred_element_type=f32)


def shifted(value, axis, steps):
    count = lax.axis_size(axis)
    pairs = [(source, (source + steps) % count) for source in range(count)]
    return lax.ppermute(value, axis, pairs)


def product_kernel(w_hbm, q_hbm, pack_ref, w_ref, q_ref, sems):
    width, cols = w_ref.shape
    w_copy = pltpu.make_async_copy(w_hbm, w_ref, sems.at[0])
    q_copy = pltpu.make_async_copy(q_hbm, q_ref, sems.at[1])
    w_copy.start()
    q_copy.start()
    q_copy.wait()
    q = q_ref[...]
    pack_ref[:, pl.ds(width, cols)] = q.astype(f32)
    w_copy.wait()
    pack_ref[:, :width] = dot(q, w_ref[...], ((1,), (1,)))


def partial_kernel(pack_ref, w_ref, out_ref):
    width, cols = w_ref.shape
    q = pack_ref[:, pl.ds(width, cols)].astype(bf16)
    part = (pack_ref[:, :width] - dot(q, w_ref[...], ((1,), (1,)))).astype(bf16)
    for copy in range(out_ref.shape[0]):
        out_ref[copy] = part


def inverse_factor(gram):
    rank = gram.shape[0]
    shape = (rank, 128)
    lane = lax.broadcasted_iota(jnp.int32, shape, 1)
    row = lax.broadcasted_iota(jnp.int32, shape, 0)
    left = [jnp.broadcast_to(gram[:, j : j + 1], shape) for j in range(rank)]
    right = [jnp.zeros(shape, f32) for j in range(rank)]
    pivots = jnp.ones(shape, f32)
    for k in range(rank):
        pivot = jnp.broadcast_to(left[k][k : k + 1], shape)
        pivots = jnp.where(row == k, pivot, pivots)
        right[k] = jnp.where(row == k, 1.0, 0.0).astype(f32)
        if k == rank - 1:
            break
        factor = jnp.where(row > k, left[k] / pivot, 0.0)
        for j in range(k + 1, rank):
            left[j] = left[j] - factor * jnp.broadcast_to(left[j][k : k + 1], shape)
        for j in range(k):
            right[j] = right[j] - factor * jnp.broadcast_to(right[j][k : k + 1], shape)
        right[k] = right[k] - factor
    gathered = jnp.zeros(shape, f32)
    for j in range(rank):
        gathered = jnp.where(lane % rank == j, right[j], gathered)
    return gathered / jnp.sqrt(pivots)


def basis_kernel(g_ref, basis_ref):
    rank = basis_ref.shape[0]
    diff = g_ref[0].astype(f32)
    for peer in range(1, g_ref.shape[0]):
        diff = diff + g_ref[peer].astype(f32)
    high = diff.astype(bf16)
    low = (diff - high.astype(f32)).astype(bf16)
    gram = (
        dot(high, high, ((1,), (1,)))
        + dot(high, low, ((1,), (1,)))
        + dot(low, high, ((1,), (1,)))
    )
    inverse = inverse_factor(gram)
    lane = lax.broadcasted_iota(jnp.int32, inverse.shape, 1)
    coarse = inverse.astype(bf16).astype(f32)
    mix = jnp.where(lane < 2 * rank, coarse, inverse - coarse)[:, : 4 * rank].astype(bf16)
    terms = jnp.concatenate([high, low, high, low], 0)
    basis_ref[...] = dot(mix, terms, ((1,), (0,))).astype(bf16)


def image_kernel(basis_ref, wl_ref, w_ref, pack_ref):
    width, cols = w_ref.shape
    basis = basis_ref[...]
    pack_ref[:, :width] = basis
    image = dot(basis, wl_ref[...], ((1,), (0,))) - dot(basis, w_ref[...], ((1,), (0,)))
    for term in range(3):
        piece = image.astype(bf16)
        pack_ref[:, pl.ds(width + term * cols, cols)] = piece
        image = image - piece.astype(f32)


def update_kernel(left_ref, right_ref, pre_ref, new_hbm, next_hbm, new_ref, next_ref, sems):
    width, cols = new_ref.shape
    terms = [pl.ds(width + term * cols, cols) for term in range(3)]
    pieces = [right_ref[:, t] for t in terms]
    next_ref[...] = (
        pieces[0].astype(f32) + pieces[1].astype(f32) + pieces[2].astype(f32)
    )
    copies = [pltpu.make_async_copy(next_ref, next_hbm, sems.at[0])]
    copies[0].start()
    nexts = jnp.concatenate(pieces + [-left_ref[:, t] for t in terms], 0)
    tile = 512
    for start in range(0, width, tile):
        rows = pl.ds(start, tile)
        left, right = left_ref[:, rows], right_ref[:, rows]
        lhs = jnp.concatenate([right, right, right, left, left, left], 0)
        correction = dot(lhs, nexts, ((0,), (0,)))
        new_ref[rows] = (pre_ref[rows] - gossip_rate * correction).astype(bf16)
        copies.append(
            pltpu.make_async_copy(new_ref.at[rows], new_hbm.at[rows], sems.at[len(copies)])
        )
        copies[-1].start()
    for copy in copies:
        copy.wait()


def body(weights, grads, first_moment, second_moment, vectors):
    weight = weights[0]
    rows, cols = weight.shape
    rank = vectors.shape[1]
    peers = lax.axis_size("tensor")
    vmem = pl.BlockSpec(memory_space=pltpu.VMEM)
    hbm = pl.BlockSpec(memory_space=pltpu.HBM)
    shaped = jax.ShapeDtypeStruct

    def call(kernel, name, out_shape, *operands):
        return pl.pallas_call(
            kernel,
            out_shape=out_shape,
            in_specs=[vmem] * len(operands),
            out_specs=jax.tree.map(lambda _: vmem, out_shape),
            compiler_params=pltpu.CompilerParams(vmem_limit_bytes=8 * 1024 * 1024),
            cost_estimate=pl.CostEstimate(
                flops=10_000_000, bytes_accessed=4_000_000, transcendentals=500_000
            ),
            name=name,
        )(*operands)

    product, w_here = pl.pallas_call(
        product_kernel,
        out_shape=(
            pltpu.VMEM((rank, rows + cols), f32),
            pltpu.VMEM((rows, cols), bf16),
        ),
        in_specs=[hbm, hbm],
        out_specs=(vmem, vmem),
        scratch_shapes=[pltpu.VMEM((rank, cols), bf16), pltpu.SemaphoreType.DMA((2,))],
        compiler_params=pltpu.CompilerParams(vmem_limit_bytes=8 * 1024 * 1024),
        cost_estimate=pl.CostEstimate(
            flops=10_000_000, bytes_accessed=4_000_000, transcendentals=0
        ),
        name="own_product",
    )(
        pltpu.with_memory_space_constraint(weight, pltpu.HBM),
        pltpu.with_memory_space_constraint(vectors[0], pltpu.HBM),
    )
    left_product = shifted(product, "blk", 1)
    w_left = shifted(w_here, "blk", 1)
    partials = call(
        partial_kernel,
        "partial_differences",
        shaped((peers, rank, rows), bf16),
        left_product,
        w_here,
    )
    gathered = lax.all_to_all(partials, "tensor", 0, 0)
    basis = call(basis_kernel, "basis", shaped((rank, rows), bf16), gathered)
    pack = call(
        image_kernel, "image", shaped((rank, rows + 3 * cols), bf16), basis, w_left, w_here
    )
    right_pack = shifted(pack, "blk", -1)

    wide = w_here.astype(f32)
    gfull = grads[0].astype(f32)
    first = beta_one * first_moment[0] + (1.0 - beta_one) * gfull
    second = beta_two * second_moment[0] + (1.0 - beta_two) * gfull * gfull
    step = first / bias_one / (jnp.sqrt(second / bias_two) + epsilon) + decay_rate * wide
    pre = wide - learn_rate * step

    new, next_right = pl.pallas_call(
        update_kernel,
        out_shape=(shaped((rows, cols), bf16), shaped((rank, cols), f32)),
        in_specs=[vmem] * 3,
        out_specs=(hbm, hbm),
        scratch_shapes=[
            pltpu.VMEM((rows, cols), bf16),
            pltpu.VMEM((rank, cols), f32),
            pltpu.SemaphoreType.DMA((1 + rows // 512,)),
        ],
        compiler_params=pltpu.CompilerParams(vmem_limit_bytes=8 * 1024 * 1024),
        cost_estimate=pl.CostEstimate(
            flops=10_000_000, bytes_accessed=4_000_000, transcendentals=0
        ),
        name="update",
    )(pack, right_pack, pre)
    return (new[None], next_right[None])


def solution(mesh):
    spec = P("blk", None, "tensor")
    return jax.shard_map(
        body,
        mesh=mesh,
        in_specs=(spec,) * 5,
        out_specs=(spec, spec),
        check_vma=False,
    )
```

```python
import jax
import jax.numpy as jnp
from jax import lax
from jax.experimental import pallas as pl
from jax.experimental.pallas import tpu as pltpu
from jax.sharding import PartitionSpec as P

learn_rate = 0.05
beta_one = 0.9
beta_two = 0.95
epsilon = 1e-08
decay_rate = 0.1
gossip_rate = 0.5
bias_one = 1.0 - 0.9**10
bias_two = 1.0 - 0.95**10

f32 = jnp.float32
bf16 = jnp.bfloat16


def dot(a, b, dims):
    return lax.dot_general(a, b, (dims, ((), ())), preferred_element_type=f32)


def shifted(value, axis, steps):
    count = lax.axis_size(axis)
    pairs = [(source, (source + steps) % count) for source in range(count)]
    return lax.ppermute(value, axis, pairs)


def product_kernel(w_hbm, q_hbm, pack_ref, w_ref, q_ref, sems):
    width, cols = w_ref.shape
    w_copy = pltpu.make_async_copy(w_hbm, w_ref, sems.at[0])
    q_copy = pltpu.make_async_copy(q_hbm, q_ref, sems.at[1])
    w_copy.start()
    q_copy.start()
    q_copy.wait()
    q = q_ref[...]
    pack_ref[:, pl.ds(width, cols)] = q.astype(f32)
    w_copy.wait()
    pack_ref[:, :width] = dot(q, w_ref[...], ((1,), (1,)))


def partial_kernel(pack_ref, w_ref, out_ref):
    width, cols = w_ref.shape
    q = pack_ref[:, pl.ds(width, cols)].astype(bf16)
    part = (pack_ref[:, :width] - dot(q, w_ref[...], ((1,), (1,)))).astype(bf16)
    for copy in range(out_ref.shape[0]):
        out_ref[copy] = part


def inverse_factor(gram):
    rank = gram.shape[0]
    shape = (rank, 128)
    lane = lax.broadcasted_iota(jnp.int32, shape, 1)
    row = lax.broadcasted_iota(jnp.int32, shape, 0)
    left = [jnp.broadcast_to(gram[:, j : j + 1], shape) for j in range(rank)]
    right = [jnp.zeros(shape, f32) for j in range(rank)]
    pivots = jnp.ones(shape, f32)
    for k in range(rank):
        pivot = jnp.broadcast_to(left[k][k : k + 1], shape)
        pivots = jnp.where(row == k, pivot, pivots)
        right[k] = jnp.where(row == k, 1.0, 0.0).astype(f32)
        if k == rank - 1:
            break
        factor = jnp.where(row > k, left[k] / pivot, 0.0)
        for j in range(k + 1, rank):
            left[j] = left[j] - factor * jnp.broadcast_to(left[j][k : k + 1], shape)
        for j in range(k):
            right[j] = right[j] - factor * jnp.broadcast_to(right[j][k : k + 1], shape)
        right[k] = right[k] - factor
    gathered = jnp.zeros(shape, f32)
    for j in range(rank):
        gathered = jnp.where(lane % rank == j, right[j], gathered)
    return gathered / jnp.sqrt(pivots)


def basis_kernel(g_ref, basis_ref):
    rank = basis_ref.shape[0]
    diff = g_ref[0].astype(f32)
    for peer in range(1, g_ref.shape[0]):
        diff = diff + g_ref[peer].astype(f32)
    high = diff.astype(bf16)
    low = (diff - high.astype(f32)).astype(bf16)
    gram = (
        dot(high, high, ((1,), (1,)))
        + dot(high, low, ((1,), (1,)))
        + dot(low, high, ((1,), (1,)))
    )
    inverse = inverse_factor(gram)
    lane = lax.broadcasted_iota(jnp.int32, inverse.shape, 1)
    coarse = inverse.astype(bf16).astype(f32)
    mix = jnp.where(lane < 2 * rank, coarse, inverse - coarse)[:, : 4 * rank].astype(bf16)
    terms = jnp.concatenate([high, low, high, low], 0)
    basis_ref[...] = dot(mix, terms, ((1,), (0,))).astype(bf16)


def image_kernel(basis_ref, wl_ref, w_ref, pack_ref):
    width, cols = w_ref.shape
    basis = basis_ref[...]
    pack_ref[:, :width] = basis
    image = dot(basis, wl_ref[...], ((1,), (0,))) - dot(basis, w_ref[...], ((1,), (0,)))
    for term in range(3):
        piece = image.astype(bf16)
        pack_ref[:, pl.ds(width + term * cols, cols)] = piece
        image = image - piece.astype(f32)


def update_kernel(left_ref, right_ref, pre_ref, new_hbm, next_hbm, new_ref, next_ref, sems):
    width, cols = new_ref.shape
    terms = [pl.ds(width + term * cols, cols) for term in range(3)]
    pieces = [right_ref[:, t] for t in terms]
    next_ref[...] = (
        pieces[0].astype(f32) + pieces[1].astype(f32) + pieces[2].astype(f32)
    )
    copies = [pltpu.make_async_copy(next_ref, next_hbm, sems.at[0])]
    copies[0].start()
    nexts = jnp.concatenate(pieces + [-left_ref[:, t] for t in terms], 0)
    tile = 512
    for start in range(0, width, tile):
        rows = pl.ds(start, tile)
        left, right = left_ref[:, rows], right_ref[:, rows]
        lhs = jnp.concatenate([right, right, right, left, left, left], 0)
        correction = dot(lhs, nexts, ((0,), (0,)))
        new_ref[rows] = (pre_ref[rows] - gossip_rate * correction).astype(bf16)
        copies.append(
            pltpu.make_async_copy(new_ref.at[rows], new_hbm.at[rows], sems.at[len(copies)])
        )
        copies[-1].start()
    for copy in copies:
        copy.wait()


def body(weights, grads, first_moment, second_moment, vectors):
    weight = weights[0]
    rows, cols = weight.shape
    rank = vectors.shape[1]
    peers = lax.axis_size("tensor")
    vmem = pl.BlockSpec(memory_space=pltpu.VMEM)
    hbm = pl.BlockSpec(memory_space=pltpu.HBM)
    shaped = jax.ShapeDtypeStruct

    def call(kernel, name, out_shape, *operands):
        return pl.pallas_call(
            kernel,
            out_shape=out_shape,
            in_specs=[vmem] * len(operands),
            out_specs=jax.tree.map(lambda _: vmem, out_shape),
            compiler_params=pltpu.CompilerParams(vmem_limit_bytes=8 * 1024 * 1024),
            cost_estimate=pl.CostEstimate(
                flops=10_000_000, bytes_accessed=4_000_000, transcendentals=500_000
            ),
            name=name,
        )(*operands)

    product, w_here = pl.pallas_call(
        product_kernel,
        out_shape=(
            pltpu.VMEM((rank, rows + cols), f32),
            pltpu.VMEM((rows, cols), bf16),
        ),
        in_specs=[hbm, hbm],
        out_specs=(vmem, vmem),
        scratch_shapes=[pltpu.VMEM((rank, cols), bf16), pltpu.SemaphoreType.DMA((2,))],
        compiler_params=pltpu.CompilerParams(vmem_limit_bytes=8 * 1024 * 1024),
        cost_estimate=pl.CostEstimate(
            flops=10_000_000, bytes_accessed=4_000_000, transcendentals=0
        ),
        name="own_product",
    )(
        pltpu.with_memory_space_constraint(weight, pltpu.HBM),
        pltpu.with_memory_space_constraint(vectors[0], pltpu.HBM),
    )
    left_product = shifted(product, "blk", 1)
    w_left = shifted(w_here, "blk", 1)
    partials = call(
        partial_kernel,
        "partial_differences",
        shaped((peers, rank, rows), bf16),
        left_product,
        w_here,
    )
    order = list(range(peers // 2)) + list(range(peers - 1, peers // 2 - 1, -1))
    gathered = lax.all_to_all(partials, "tensor", 0, 0, axis_index_groups=[order])
    basis = call(basis_kernel, "basis", shaped((rank, rows), bf16), gathered)
    pack = call(
        image_kernel, "image", shaped((rank, rows + 3 * cols), bf16), basis, w_left, w_here
    )
    right_pack = shifted(pack, "blk", -1)

    wide = w_here.astype(f32)
    gfull = grads[0].astype(f32)
    first = beta_one * first_moment[0] + (1.0 - beta_one) * gfull
    second = beta_two * second_moment[0] + (1.0 - beta_two) * gfull * gfull
    step = first / bias_one / (jnp.sqrt(second / bias_two) + epsilon) + decay_rate * wide
    pre = wide - learn_rate * step

    new, next_right = pl.pallas_call(
        update_kernel,
        out_shape=(shaped((rows, cols), bf16), shaped((rank, cols), f32)),
        in_specs=[vmem] * 3,
        out_specs=(hbm, hbm),
        scratch_shapes=[
            pltpu.VMEM((rows, cols), bf16),
            pltpu.VMEM((rank, cols), f32),
            pltpu.SemaphoreType.DMA((1 + rows // 512,)),
        ],
        compiler_params=pltpu.CompilerParams(vmem_limit_bytes=8 * 1024 * 1024),
        cost_estimate=pl.CostEstimate(
            flops=10_000_000, bytes_accessed=4_000_000, transcendentals=0
        ),
        name="update",
    )(pack, right_pack, pre)
    return (new[None], next_right[None])


def solution(mesh):
    spec = P("blk", None, "tensor")
    return jax.shard_map(
        body,
        mesh=mesh,
        in_specs=(spec,) * 5,
        out_specs=(spec, spec),
        check_vma=False,
    )
```

```python
import jax
import jax.numpy as jnp
from jax import lax
from jax.experimental import pallas as pl
from jax.experimental.pallas import tpu as pltpu
from jax.sharding import PartitionSpec as P

learn_rate = 0.05
beta_one = 0.9
beta_two = 0.95
epsilon = 1e-08
decay_rate = 0.1
gossip_rate = 0.5
bias_one = 1.0 - 0.9**10
bias_two = 1.0 - 0.95**10

f32 = jnp.float32
bf16 = jnp.bfloat16


def dot(a, b, dims):
    return lax.dot_general(a, b, (dims, ((), ())), preferred_element_type=f32)


def shifted(value, axis, steps):
    count = lax.axis_size(axis)
    pairs = [(source, (source + steps) % count) for source in range(count)]
    return lax.ppermute(value, axis, pairs)


def product_kernel(w_hbm, q_hbm, pack_ref, w_ref, q_ref, sems):
    width, cols = w_ref.shape
    w_copy = pltpu.make_async_copy(w_hbm, w_ref, sems.at[0])
    q_copy = pltpu.make_async_copy(q_hbm, q_ref, sems.at[1])
    w_copy.start()
    q_copy.start()
    q_copy.wait()
    q = q_ref[...]
    pack_ref[:, pl.ds(width, cols)] = q.astype(f32)
    w_copy.wait()
    pack_ref[:, :width] = dot(q, w_ref[...], ((1,), (1,)))


def partial_kernel(pack_ref, w_ref, out_ref):
    width, cols = w_ref.shape
    q = pack_ref[:, pl.ds(width, cols)].astype(bf16)
    part = (pack_ref[:, :width] - dot(q, w_ref[...], ((1,), (1,)))).astype(bf16)
    for copy in range(out_ref.shape[0]):
        out_ref[copy] = part


def inverse_factor(gram):
    rank = gram.shape[0]
    shape = (rank, 128)
    lane = lax.broadcasted_iota(jnp.int32, shape, 1)
    row = lax.broadcasted_iota(jnp.int32, shape, 0)
    left = [jnp.broadcast_to(gram[:, j : j + 1], shape) for j in range(rank)]
    right = [jnp.zeros(shape, f32) for j in range(rank)]
    pivots = jnp.ones(shape, f32)
    for k in range(rank):
        pivot = jnp.broadcast_to(left[k][k : k + 1], shape)
        pivots = jnp.where(row == k, pivot, pivots)
        right[k] = jnp.where(row == k, 1.0, 0.0).astype(f32)
        if k == rank - 1:
            break
        factor = jnp.where(row > k, left[k] / pivot, 0.0)
        for j in range(k + 1, rank):
            left[j] = left[j] - factor * jnp.broadcast_to(left[j][k : k + 1], shape)
        for j in range(k):
            right[j] = right[j] - factor * jnp.broadcast_to(right[j][k : k + 1], shape)
        right[k] = right[k] - factor
    gathered = jnp.zeros(shape, f32)
    for j in range(rank):
        gathered = jnp.where(lane % rank == j, right[j], gathered)
    return gathered / jnp.sqrt(pivots)


def basis_kernel(g_ref, basis_ref):
    rank = basis_ref.shape[0]
    diff = g_ref[0].astype(f32)
    for peer in range(1, g_ref.shape[0]):
        diff = diff + g_ref[peer].astype(f32)
    high = diff.astype(bf16)
    low = (diff - high.astype(f32)).astype(bf16)
    gram = (
        dot(high, high, ((1,), (1,)))
        + dot(high, low, ((1,), (1,)))
        + dot(low, high, ((1,), (1,)))
    )
    inverse = inverse_factor(gram)
    lane = lax.broadcasted_iota(jnp.int32, inverse.shape, 1)
    coarse = inverse.astype(bf16).astype(f32)
    mix = jnp.where(lane < 2 * rank, coarse, inverse - coarse)[:, : 4 * rank].astype(bf16)
    terms = jnp.concatenate([high, low, high, low], 0)
    basis_ref[...] = dot(mix, terms, ((1,), (0,))).astype(bf16)


def image_kernel(basis_ref, wl_ref, w_ref, pack_ref):
    width, cols = w_ref.shape
    basis = basis_ref[...]
    pack_ref[:, :width] = basis
    image = dot(basis, wl_ref[...], ((1,), (0,))) - dot(basis, w_ref[...], ((1,), (0,)))
    for term in range(3):
        piece = image.astype(bf16)
        pack_ref[:, pl.ds(width + term * cols, cols)] = piece
        image = image - piece.astype(f32)


def left_kernel(left_ref, pre_ref, out_ref):
    width, cols = out_ref.shape
    nexts = jnp.concatenate(
        [left_ref[:, pl.ds(width + term * cols, cols)] for term in range(3)], 0
    )
    tile = 512
    for start in range(0, width, tile):
        rows = pl.ds(start, tile)
        left = left_ref[:, rows]
        lhs = jnp.concatenate([left, left, left], 0)
        out_ref[rows] = pre_ref[rows] + gossip_rate * dot(lhs, nexts, ((0,), (0,)))


def update_kernel(right_ref, pre_ref, new_hbm, next_hbm, new_ref, next_ref, sems):
    width, cols = new_ref.shape
    pieces = [right_ref[:, pl.ds(width + term * cols, cols)] for term in range(3)]
    next_ref[...] = (
        pieces[0].astype(f32) + pieces[1].astype(f32) + pieces[2].astype(f32)
    )
    copies = [pltpu.make_async_copy(next_ref, next_hbm, sems.at[0])]
    copies[0].start()
    nexts = jnp.concatenate(pieces, 0)
    tile = 512
    for start in range(0, width, tile):
        rows = pl.ds(start, tile)
        right = right_ref[:, rows]
        lhs = jnp.concatenate([right, right, right], 0)
        correction = dot(lhs, nexts, ((0,), (0,)))
        new_ref[rows] = (pre_ref[rows] - gossip_rate * correction).astype(bf16)
        copies.append(
            pltpu.make_async_copy(new_ref.at[rows], new_hbm.at[rows], sems.at[len(copies)])
        )
        copies[-1].start()
    for copy in copies:
        copy.wait()


def body(weights, grads, first_moment, second_moment, vectors):
    weight = weights[0]
    rows, cols = weight.shape
    rank = vectors.shape[1]
    peers = lax.axis_size("tensor")
    vmem = pl.BlockSpec(memory_space=pltpu.VMEM)
    hbm = pl.BlockSpec(memory_space=pltpu.HBM)
    shaped = jax.ShapeDtypeStruct

    def call(kernel, name, out_shape, *operands):
        return pl.pallas_call(
            kernel,
            out_shape=out_shape,
            in_specs=[vmem] * len(operands),
            out_specs=jax.tree.map(lambda _: vmem, out_shape),
            compiler_params=pltpu.CompilerParams(vmem_limit_bytes=8 * 1024 * 1024),
            cost_estimate=pl.CostEstimate(
                flops=10_000_000, bytes_accessed=4_000_000, transcendentals=500_000
            ),
            name=name,
        )(*operands)

    product, w_here = pl.pallas_call(
        product_kernel,
        out_shape=(
            pltpu.VMEM((rank, rows + cols), f32),
            pltpu.VMEM((rows, cols), bf16),
        ),
        in_specs=[hbm, hbm],
        out_specs=(vmem, vmem),
        scratch_shapes=[pltpu.VMEM((rank, cols), bf16), pltpu.SemaphoreType.DMA((2,))],
        compiler_params=pltpu.CompilerParams(vmem_limit_bytes=8 * 1024 * 1024),
        cost_estimate=pl.CostEstimate(
            flops=10_000_000, bytes_accessed=4_000_000, transcendentals=0
        ),
        name="own_product",
    )(
        pltpu.with_memory_space_constraint(weight, pltpu.HBM),
        pltpu.with_memory_space_constraint(vectors[0], pltpu.HBM),
    )
    left_product = shifted(product, "blk", 1)
    w_left = shifted(w_here, "blk", 1)
    partials = call(
        partial_kernel,
        "partial_differences",
        shaped((peers, rank, rows), bf16),
        left_product,
        w_here,
    )
    order = list(range(peers // 2)) + list(range(peers - 1, peers // 2 - 1, -1))
    gathered = lax.all_to_all(partials, "tensor", 0, 0, axis_index_groups=[order])
    basis = call(basis_kernel, "basis", shaped((rank, rows), bf16), gathered)
    pack = call(
        image_kernel, "image", shaped((rank, rows + 3 * cols), bf16), basis, w_left, w_here
    )
    right_pack = shifted(pack, "blk", -1)

    wide = w_here.astype(f32)
    gfull = grads[0].astype(f32)
    first = beta_one * first_moment[0] + (1.0 - beta_one) * gfull
    second = beta_two * second_moment[0] + (1.0 - beta_two) * gfull * gfull
    step = first / bias_one / (jnp.sqrt(second / bias_two) + epsilon) + decay_rate * wide
    pre = wide - learn_rate * step

    pre = call(left_kernel, "left_correction", shaped((rows, cols), f32), pack, pre)
    new, next_right = pl.pallas_call(
        update_kernel,
        out_shape=(shaped((rows, cols), bf16), shaped((rank, cols), f32)),
        in_specs=[vmem] * 2,
        out_specs=(hbm, hbm),
        scratch_shapes=[
            pltpu.VMEM((rows, cols), bf16),
            pltpu.VMEM((rank, cols), f32),
            pltpu.SemaphoreType.DMA((1 + rows // 512,)),
        ],
        compiler_params=pltpu.CompilerParams(vmem_limit_bytes=8 * 1024 * 1024),
        cost_estimate=pl.CostEstimate(
            flops=10_000_000, bytes_accessed=4_000_000, transcendentals=0
        ),
        name="update",
    )(right_pack, pre)
    return (new[None], next_right[None])


def solution(mesh):
    spec = P("blk", None, "tensor")
    return jax.shard_map(
        body,
        mesh=mesh,
        in_specs=(spec,) * 5,
        out_specs=(spec, spec),
        check_vma=False,
    )
```

```python
import jax
import jax.numpy as jnp
from jax import lax
from jax.experimental import pallas as pl
from jax.experimental.pallas import tpu as pltpu
from jax.sharding import PartitionSpec as P

learn_rate = 0.05
beta_one = 0.9
beta_two = 0.95
epsilon = 1e-08
decay_rate = 0.1
gossip_rate = 0.5
bias_one = 1.0 - 0.9**10
bias_two = 1.0 - 0.95**10

f32 = jnp.float32
bf16 = jnp.bfloat16


def dot(a, b, dims):
    return lax.dot_general(a, b, (dims, ((), ())), preferred_element_type=f32)


def shifted(value, axis, steps):
    count = lax.axis_size(axis)
    pairs = [(source, (source + steps) % count) for source in range(count)]
    return lax.ppermute(value, axis, pairs)


def product_kernel(w_hbm, q_hbm, pack_ref, w_ref, q_ref, sems):
    width, cols = w_ref.shape
    w_copy = pltpu.make_async_copy(w_hbm, w_ref, sems.at[0])
    q_copy = pltpu.make_async_copy(q_hbm, q_ref, sems.at[1])
    w_copy.start()
    q_copy.start()
    q_copy.wait()
    q = q_ref[...]
    pack_ref[:, pl.ds(width, cols)] = q.astype(f32)
    w_copy.wait()
    pack_ref[:, :width] = dot(q, w_ref[...], ((1,), (1,)))


def partial_kernel(pack_ref, w_ref, out_ref):
    width, cols = w_ref.shape
    q = pack_ref[:, pl.ds(width, cols)].astype(bf16)
    part = (pack_ref[:, :width] - dot(q, w_ref[...], ((1,), (1,)))).astype(bf16)
    for copy in range(out_ref.shape[0]):
        out_ref[copy] = part


def inverse_factor(gram):
    rank = gram.shape[0]
    shape = (rank, 128)
    lane = lax.broadcasted_iota(jnp.int32, shape, 1)
    row = lax.broadcasted_iota(jnp.int32, shape, 0)
    left = [jnp.broadcast_to(gram[:, j : j + 1], shape) for j in range(rank)]
    right = [jnp.zeros(shape, f32) for j in range(rank)]
    pivots = jnp.ones(shape, f32)
    for k in range(rank):
        pivot = jnp.broadcast_to(left[k][k : k + 1], shape)
        pivots = jnp.where(row == k, pivot, pivots)
        right[k] = jnp.where(row == k, 1.0, 0.0).astype(f32)
        if k == rank - 1:
            break
        factor = jnp.where(row > k, left[k] / pivot, 0.0)
        for j in range(k + 1, rank):
            left[j] = left[j] - factor * jnp.broadcast_to(left[j][k : k + 1], shape)
        for j in range(k):
            right[j] = right[j] - factor * jnp.broadcast_to(right[j][k : k + 1], shape)
        right[k] = right[k] - factor
    gathered = jnp.zeros(shape, f32)
    for j in range(rank):
        gathered = jnp.where(lane % rank == j, right[j], gathered)
    return gathered / jnp.sqrt(pivots)


def basis_kernel(g_ref, basis_ref):
    rank = basis_ref.shape[0]
    diff = g_ref[0].astype(f32)
    for peer in range(1, g_ref.shape[0]):
        diff = diff + g_ref[peer].astype(f32)
    high = diff.astype(bf16)
    low = (diff - high.astype(f32)).astype(bf16)
    gram = (
        dot(high, high, ((1,), (1,)))
        + dot(high, low, ((1,), (1,)))
        + dot(low, high, ((1,), (1,)))
    )
    inverse = inverse_factor(gram)
    lane = lax.broadcasted_iota(jnp.int32, inverse.shape, 1)
    coarse = inverse.astype(bf16).astype(f32)
    mix = jnp.where(lane < 2 * rank, coarse, inverse - coarse)[:, : 4 * rank].astype(bf16)
    terms = jnp.concatenate([high, low, high, low], 0)
    basis_ref[...] = dot(mix, terms, ((1,), (0,))).astype(bf16)


def image_kernel(basis_ref, wl_ref, w_ref, pack_ref):
    width, cols = w_ref.shape
    basis = basis_ref[...]
    pack_ref[:, :width] = basis
    image = dot(basis, wl_ref[...], ((1,), (0,))) - dot(basis, w_ref[...], ((1,), (0,)))
    for term in range(3):
        piece = image.astype(bf16)
        pack_ref[:, pl.ds(width + term * cols, cols)] = piece
        image = image - piece.astype(f32)


def left_kernel(left_ref, pre_ref, out_ref):
    width, cols = out_ref.shape
    nexts = jnp.concatenate(
        [left_ref[:, pl.ds(width + term * cols, cols)] for term in range(3)], 0
    )
    tile = 512
    for start in range(0, width, tile):
        rows = pl.ds(start, tile)
        left = left_ref[:, rows]
        lhs = jnp.concatenate([left, left, left], 0)
        out_ref[rows] = pre_ref[rows] + gossip_rate * dot(lhs, nexts, ((0,), (0,)))


def update_kernel(right_ref, pre_ref, new_hbm, next_hbm, new_ref, next_ref, sems):
    width, cols = new_ref.shape
    pieces = [right_ref[:, pl.ds(width + term * cols, cols)] for term in range(3)]
    next_ref[...] = (
        pieces[0].astype(f32) + pieces[1].astype(f32) + pieces[2].astype(f32)
    )
    copies = [pltpu.make_async_copy(next_ref, next_hbm, sems.at[0])]
    copies[0].start()
    nexts = jnp.concatenate(pieces, 0)
    tile = 512
    for start in range(0, width, tile):
        rows = pl.ds(start, tile)
        right = right_ref[:, rows]
        lhs = jnp.concatenate([right, right, right], 0)
        correction = dot(lhs, nexts, ((0,), (0,)))
        new_ref[rows] = (pre_ref[rows] - gossip_rate * correction).astype(bf16)
        copies.append(
            pltpu.make_async_copy(new_ref.at[rows], new_hbm.at[rows], sems.at[len(copies)])
        )
        copies[-1].start()
    for copy in copies:
        copy.wait()


def body(weights, grads, first_moment, second_moment, vectors):
    weight = weights[0]
    rows, cols = weight.shape
    rank = vectors.shape[1]
    peers = lax.axis_size("tensor")
    vmem = pl.BlockSpec(memory_space=pltpu.VMEM)
    hbm = pl.BlockSpec(memory_space=pltpu.HBM)
    shaped = jax.ShapeDtypeStruct

    def call(kernel, name, out_shape, *operands):
        return pl.pallas_call(
            kernel,
            out_shape=out_shape,
            in_specs=[vmem] * len(operands),
            out_specs=jax.tree.map(lambda _: vmem, out_shape),
            compiler_params=pltpu.CompilerParams(vmem_limit_bytes=8 * 1024 * 1024),
            cost_estimate=pl.CostEstimate(
                flops=10_000_000, bytes_accessed=4_000_000, transcendentals=500_000
            ),
            name=name,
        )(*operands)

    product, w_here = pl.pallas_call(
        product_kernel,
        out_shape=(
            pltpu.VMEM((rank, rows + cols), f32),
            pltpu.VMEM((rows, cols), bf16),
        ),
        in_specs=[hbm, hbm],
        out_specs=(vmem, vmem),
        scratch_shapes=[pltpu.VMEM((rank, cols), bf16), pltpu.SemaphoreType.DMA((2,))],
        compiler_params=pltpu.CompilerParams(vmem_limit_bytes=8 * 1024 * 1024),
        cost_estimate=pl.CostEstimate(
            flops=10_000_000, bytes_accessed=4_000_000, transcendentals=0
        ),
        name="own_product",
    )(
        pltpu.with_memory_space_constraint(weight, pltpu.HBM),
        pltpu.with_memory_space_constraint(vectors[0], pltpu.HBM),
    )
    left_product = shifted(product, "blk", 1)
    w_left = shifted(w_here, "blk", 1)
    partials = call(
        partial_kernel,
        "partial_differences",
        shaped((peers, rank, rows), bf16),
        left_product,
        w_here,
    )
    order = [0, 1, 5, 4, 7, 6, 2, 3]
    gathered = lax.all_to_all(partials, "tensor", 0, 0, axis_index_groups=[order])
    basis = call(basis_kernel, "basis", shaped((rank, rows), bf16), gathered)
    pack = call(
        image_kernel, "image", shaped((rank, rows + 3 * cols), bf16), basis, w_left, w_here
    )
    right_pack = shifted(pack, "blk", -1)

    wide = w_here.astype(f32)
    gfull = grads[0].astype(f32)
    first = beta_one * first_moment[0] + (1.0 - beta_one) * gfull
    second = beta_two * second_moment[0] + (1.0 - beta_two) * gfull * gfull
    step = first / bias_one / (jnp.sqrt(second / bias_two) + epsilon) + decay_rate * wide
    pre = wide - learn_rate * step

    pre = call(left_kernel, "left_correction", shaped((rows, cols), f32), pack, pre)
    new, next_right = pl.pallas_call(
        update_kernel,
        out_shape=(shaped((rows, cols), bf16), shaped((rank, cols), f32)),
        in_specs=[vmem] * 2,
        out_specs=(hbm, hbm),
        scratch_shapes=[
            pltpu.VMEM((rows, cols), bf16),
            pltpu.VMEM((rank, cols), f32),
            pltpu.SemaphoreType.DMA((1 + rows // 512,)),
        ],
        compiler_params=pltpu.CompilerParams(vmem_limit_bytes=8 * 1024 * 1024),
        cost_estimate=pl.CostEstimate(
            flops=10_000_000, bytes_accessed=4_000_000, transcendentals=0
        ),
        name="update",
    )(right_pack, pre)
    return (new[None], next_right[None])


def solution(mesh):
    spec = P("blk", None, "tensor")
    return jax.shard_map(
        body,
        mesh=mesh,
        in_specs=(spec,) * 5,
        out_specs=(spec, spec),
        check_vma=False,
    )
```
